128 devices in a mesh: grid: 32 (over y, z, core), member: 4 (over x).
Axes of the slice: x: 4, y: 4, z: 4, core: 2. Of those that a mesh axis runs over, the one named last changes fastest.
Arguments:
- basis: float32 [131072, 1024], P('grid', 'member'), may hold values from -6 to 6
- scales: float32 [1024], P('member'), may hold values from 0.3 to 3
- area: float32 [131072], P('grid'), may hold values from 0.3 to 1
Outputs:
- merged_basis: float32 [131072, 256], P('grid', 'member')
The draws below stay inside these ranges and needn't reach their ends.
All inputs are finite; a program needn't handle non-finite values.
Results may differ from the reference program's by a relative error of at most 0.0003.
Values sent between devices are 32-bit elements; how exact they have to be, the bound alone decides.
A program may use at most 128 MiB of HBM per device.

```python
import math
import jax
import jax.numpy as jnp
from jax import lax

K = 256
ITERS = 3
GROUPS = 4
NPOINTS = 131072


def levels(own_key, dims, pieces, smallest, largest):
    def one(position, shards_of):
        steps = jax.random.uniform(jax.random.fold_in(jax.random.fold_in(own_key, 6), position), (shards_of,), jnp.float32, smallest / len(pieces), largest / len(pieces))
        return jnp.repeat(jnp.exp(steps), dims[position] // shards_of).reshape((-1,) + (1,) * (len(dims) - position - 1))

    loudness = one(*pieces[0])
    for cut in pieces[1:]:
        loudness = loudness * one(*cut)
    return loudness


def scatter_about(key, extent, deviation, reach, shards=(), held_as=jnp.bfloat16):
    loudness = levels(key, extent, shards, -0.22, 0.18) if shards else 1.0
    array = jax.random.normal(key, extent, jnp.float32) * deviation * loudness
    return jnp.minimum(jnp.maximum(array, -reach), reach).astype(held_as)


def setup_inputs(seed: int = 0) -> dict:
    seeds = jax.random.split(jax.random.key(seed), 4)
    basis = scatter_about(seeds[0], (NPOINTS, GROUPS * K), 1.0, 6.0, ((0, 32), (1, 4)), jnp.float32)
    scales = jnp.clip(jnp.exp(math.log(3.0) - 2.3025851 * jax.random.uniform(seeds[1], (GROUPS * K,), jnp.float32) ** levels(seeds[1], (GROUPS * K,), ((0, 4),), -0.2, 0.2)), 0.3, 3.0)
    area = jnp.clip(jnp.exp(math.log(1.0) - 1.2039728 * jax.random.uniform(seeds[2], (NPOINTS,), jnp.float32) ** levels(seeds[2], (NPOINTS,), ((0, 32),), -0.2, 0.2)), 0.3, 1.0)
    return {"basis": basis, "scales": scales, "area": area}


def orthonormal(gram, rank):
    vectors = jnp.eye(gram.shape[0], rank, dtype=jnp.float32)
    for step in range(ITERS):
        image = jnp.dot(gram, vectors, precision=lax.Precision.HIGHEST)
        square = jnp.dot(image.T, image, precision=lax.Precision.HIGHEST)
        factor = jnp.linalg.cholesky(square)
        vectors = lax.linalg.triangular_solve(factor, image, left_side=False, lower=True, transpose_a=True)
    return vectors

def merge(lower, upper):
    stacked = jnp.concatenate([lower, upper], axis=1)
    gram = jnp.dot(stacked.T, stacked, precision=lax.Precision.HIGHEST) / NPOINTS
    vectors = orthonormal(gram, lower.shape[1])
    return jnp.dot(stacked, vectors, precision=lax.Precision.HIGHEST)

def reference(basis, scales, area):
    weighted = area[:, None] * basis * scales[None, :]
    blocks = [weighted[:, g * K:(g + 1) * K] for g in range(GROUPS)]
    first = merge(blocks[0], blocks[1])
    second = merge(blocks[2], blocks[3])
    return merge(first, second)
```

```python
import jax
import jax.numpy as jnp
from jax import lax
from jax.experimental import pallas as pl
from jax.experimental.pallas import tpu as pltpu
from jax.sharding import PartitionSpec as P
HI=lax.Precision.HIGHEST
NB=64
def split(x):
    h=x.astype(jnp.bfloat16)
    return h,(x-h.astype(jnp.float32)).astype(jnp.bfloat16)
def mm(a,b,dims):
    if MODE==6:
        return lax.dot_general(a,b,(dims,((),())),precision=HI,preferred_element_type=jnp.float32)
    ah,al=split(a); bh,bl=split(b)
    d=lambda p,q: lax.dot_general(p,q,(dims,((),())),preferred_element_type=jnp.float32)
    return d(ah,bh)+(d(ah,bl)+d(al,bh))
MODE=6
nn=lambda a,b: mm(a,b,((1,),(0,)))
nt=lambda a,b: mm(a,b,((1,),(1,)))

def eliminate(mats):
    eye=(lax.broadcasted_iota(jnp.int32,(NB,NB),0)==lax.broadcasted_iota(jnp.int32,(NB,NB),1)).astype(jnp.float32)
    work=[jnp.concatenate([m,eye],axis=1) for m in mats]
    done=[[] for _ in mats]
    for k in range(NB//8):
        for b in range(len(mats)):
            s=work[b]
            rows=[s[m:m+1,:] for m in range(8)]
            cols=[jnp.broadcast_to(s[:,8*k+m:8*k+m+1],s.shape) for m in range(8)]
            for j in range(8):
                p=lax.rsqrt(cols[j][j:j+1,:])
                rows[j]=rows[j]*p
                cols[j]=cols[j]*p
                for i in range(j+1,8):
                    l=cols[j][i:i+1,:]
                    rows[i]=rows[i]-l*rows[j]
                    cols[i]=cols[i]-l*cols[j]
            done[b].append(jnp.concatenate(rows,axis=0)[:,NB:])
            if k<NB//8-1:
                t=s[8:]
                for j in range(8):
                    t=t-cols[j][8:]*rows[j]
                work[b]=t
    return [jnp.concatenate(d,axis=0) for d in done]

def inverse_factors(mats):
    n=mats[0].shape[0]
    if n==NB: return eliminate(mats)
    h=n//2
    x1=inverse_factors([a[:h,:h] for a in mats])
    l=[nt(a[h:,:h],x) for a,x in zip(mats,x1)]
    s=[a[h:,h:]-nt(q,q) for a,q in zip(mats,l)]
    x2=inverse_factors(s)
    x21=[-nn(z,nn(q,x)) for z,q,x in zip(x2,l,x1)]
    zero=jnp.zeros((h,h),jnp.float32)
    return [jnp.concatenate([jnp.concatenate([x,zero],1),jnp.concatenate([y,z],1)],0) for x,y,z in zip(x1,x21,x2)]

def bases(grams, w, p, a, x):
    n=len(grams)
    r=256
    for b in range(n):
        w[b]=grams[b][:r,:]
    def step(it,c):
        for b in range(n):
            a[b]=nt(w[b],w[b])
        xs=inverse_factors([a[b] for b in range(n)])
        for b in range(n):
            p[b]=nn(w[b],grams[b][...])
        for b in range(n): x[b]=xs[b]
        for b in range(n):
            w[b]=nn(x[b],p[b])
        return c
    lax.fori_loop(0,2,step,0)
    for b in range(n):
        a[b]=nt(w[b],w[b])
    xs=inverse_factors([a[b] for b in range(n)])
    return [nn(xs[b],w[b]) for b in range(n)]

def kernel(g_ref, out_ref, w, p, a, x, g2, u):
    gs=[g_ref.at[:512,:512], g_ref.at[512:,512:]]
    us=bases(gs,w,p,a,x)
    for b in range(2): u[b]=us[b]
    for b in range(2):
        t=nn(u[b],gs[b][...])
        g2[0,256*b:256*b+256,256*b:256*b+256]=nt(t,u[b])
    t=nt(nn(u[0],g_ref[:512,512:]),u[1])
    g2[0,:256,256:]=t
    g2[0,256:,:256]=t.T
    (v,)=bases([g2.at[0]],w,p,a,x)
    out_ref[:,:512]=nn(v[:,:256],u[0])
    out_ref[:,512:]=nn(v[:,256:],u[1])

def chain(g):
    V=lambda *s: pltpu.VMEM(s,jnp.float32)
    return pl.pallas_call(kernel,out_shape=jax.ShapeDtypeStruct((256,1024),jnp.float32),
      in_specs=[pl.BlockSpec(memory_space=pltpu.VMEM)],out_specs=pl.BlockSpec(memory_space=pltpu.VMEM),
      scratch_shapes=[V(2,256,512),V(2,256,512),V(2,256,256),V(2,256,256),V(1,512,512),V(2,256,512)],
      compiler_params=pltpu.CompilerParams(vmem_limit_bytes=48<<20))(g)


def per_device(basis, scales, area):
    npoints = basis.shape[0] * lax.axis_size("grid")
    weighted = area[:, None] * basis * scales[None, :]
    z = lax.all_to_all(weighted, "member", 0, 1, tiled=True)
    k = 256
    pairs = [(i, j) for i in range(4) for j in range(i, 4)]
    blocks = []
    for i in range(4):
        blocks.append(jnp.dot(z[:, k * i : k * i + k].T, z[:, k * i :], precision=HI))
    total = lax.psum(jnp.concatenate(blocks, axis=1), ("grid", "member")) / npoints
    rows, start = [], 0
    parts = {}
    for i in range(4):
        for j in range(i, 4):
            parts[i, j] = total[:, start : start + k]
            parts[j, i] = parts[i, j].T
            start += k
    gram = jnp.concatenate(
        [jnp.concatenate([parts[i, j] for j in range(4)], axis=1) for i in range(4)], axis=0
    )
    vectors = chain(gram)
    merged = lax.dot_general(z, vectors, (((1,), (1,)), ((), ())), precision=HI)
    return lax.all_to_all(merged, "member", 1, 0, tiled=True)


def solution(mesh):
    placed = (P("grid", "member"), P("member"), P("grid"))
    return jax.shard_map(
        per_device, mesh=mesh, in_specs=placed, out_specs=P("grid", "member"), check_vma=False
    )
```
